32 devices in a mesh: fsdp: 4 (over y, core), ctx: 4 (over z), tensor: 2 (over x).
Axes of the slice: x: 2, y: 2, z: 4, core: 2. Of those that a mesh axis runs over, the one named last changes fastest.
Arguments:
- tokens: bfloat16 [8, 1024, 2048], P('fsdp', 'ctx'), may hold values from -6 to 6
- segments: int32 [8, 1024], P('fsdp'), may hold values from 0 to 24, as said below
- cotangent: bfloat16 [8, 1024, 2048], P('fsdp', 'ctx'), may hold values from -6 to 6
- attn_gain: bfloat16 [2048], P(('fsdp', 'ctx')), may hold values from 0.5 to 1.5
- w_query: bfloat16 [2048, 2048], P(('fsdp', 'ctx'), 'tensor'), may hold values from -0.1875 to 0.1875
- w_key: bfloat16 [2048, 2048], P(('fsdp', 'ctx'), 'tensor'), may hold values from -0.1875 to 0.1875
- w_value: bfloat16 [2048, 2048], P(('fsdp', 'ctx'), 'tensor'), may hold values from -0.125 to 0.125
- w_out: bfloat16 [2048, 2048], P('tensor', ('fsdp', 'ctx')), may hold values from -0.5 to 0.5
- mlp_gain: bfloat16 [2048], P(('fsdp', 'ctx')), may hold values from 0.5 to 1.5
- w_gate: bfloat16 [2048, 8192], P(('fsdp', 'ctx'), 'tensor'), may hold values from -0.125 to 0.125
- w_up: bfloat16 [2048, 8192], P(('fsdp', 'ctx'), 'tensor'), may hold values from -0.125 to 0.125
- w_down: bfloat16 [8192, 2048], P('tensor', ('fsdp', 'ctx')), may hold values from -0.125 to 0.125
Outputs:
- block_out: bfloat16 [8, 1024, 2048], P('fsdp', 'ctx')
- grad_tokens: float32 [8, 1024, 2048], P('fsdp', 'ctx')
- grad_attn_gain: float32 [2048], P(('fsdp', 'ctx'))
- grad_query: float32 [2048, 2048], P(('fsdp', 'ctx'), 'tensor')
- grad_key: float32 [2048, 2048], P(('fsdp', 'ctx'), 'tensor')
- grad_value: float32 [2048, 2048], P(('fsdp', 'ctx'), 'tensor')
- grad_out: float32 [2048, 2048], P('tensor', ('fsdp', 'ctx'))
- grad_mlp_gain: float32 [2048], P(('fsdp', 'ctx'))
- grad_gate: float32 [2048, 8192], P(('fsdp', 'ctx'), 'tensor')
- grad_up: float32 [2048, 8192], P(('fsdp', 'ctx'), 'tensor')
- grad_down: float32 [8192, 2048], P('tensor', ('fsdp', 'ctx'))
The draws below stay inside these ranges and needn't reach their ends.
Inputs may be any that keep to these rules, and one draw needn't show every extreme that they name: `segments`: segment numbers start at 0 in every sequence and never fall; a document has 42 to 512 tokens except the last of a sequence, which may be shorter; of the 2 sequences that share one index of fsdp, one (drawn) is a single document; in one drawn index of fsdp, another of its sequences is cut into documents of exactly 42 tokens (the last may be shorter).
All inputs are finite; a program needn't handle non-finite values.
Results may differ from the reference program's by a relative error of at most 0.017.
Values may be sent and summed in bfloat16 or wider, within the bound.
No kernel may reach another device: no remote copies, remote signals or barrier semaphores. Data moves between devices by JAX's collectives and lax.ppermute only.
A program may use at most 384 MiB of HBM per device.

```python
import jax
import jax.numpy as jnp
from jax import lax

D = 2048
HEADS = 32
HEAD_DIM = 64
FF = 8192
LEN = 1024
MB = 2
SEQS = 8


def draw_segments(key, part):
    key = jax.random.fold_in(key, 11)
    key_sizes, key_pick, key_group = jax.random.split(key, 3)
    short_len = LEN // 24
    doc_count = LEN // short_len + 2
    sizes = jax.random.randint(key_sizes, (SEQS, doc_count), short_len, LEN // 2 + 1)
    ends = jnp.cumsum(sizes, axis=1)
    places = jnp.arange(LEN, dtype=jnp.int32)
    numbers = jnp.sum((ends[:, None, :] <= places[None, :, None]).astype(jnp.int32), axis=2)
    picked = jax.random.randint(key_pick, (SEQS // MB, 1), 0, MB)
    whole_doc = (jnp.arange(MB, dtype=jnp.int32)[None, :] == picked).reshape(SEQS)
    group = jax.random.randint(key_group, (), 0, SEQS // MB)
    seq_group = jnp.arange(SEQS, dtype=jnp.int32) // MB
    fine_seq = (seq_group == group) & jnp.logical_not(whole_doc)
    fine_numbers = jnp.broadcast_to((places // short_len)[None, :], (SEQS, LEN))
    numbers = jnp.where(fine_seq[:, None], fine_numbers, numbers)
    return jnp.where(whole_doc[:, None], jnp.zeros_like(numbers), numbers).astype(jnp.int32)


def block_scale(stream_key, shape, cuts, least, high):
    factor_of, own = 1.0, jax.random.fold_in(stream_key, 6)
    for position, shards_of in cuts:
        heights = jnp.exp(jax.random.uniform(jax.random.fold_in(own, position), (shards_of,), jnp.float32, least / len(cuts), high / len(cuts)))
        factor_of = factor_of * jnp.repeat(heights, shape[position] // shards_of).reshape([-1 if axis == position else 1 for axis in range(len(shape))])
    return factor_of


def centred(own_key, shape, scale, bound, pieces=(), held_as=jnp.bfloat16):
    level = block_scale(own_key, shape, pieces, -0.22, 0.18) if pieces else 1.0
    entries = jax.random.normal(own_key, shape, jnp.float32) * scale * level
    return jnp.minimum(jnp.maximum(entries, -bound), bound).astype(held_as)


def setup_inputs(seed: int = 0) -> dict:
    arg_keys = jax.random.split(jax.random.key(seed), 13)
    return {
        "tokens": centred(arg_keys[0], (SEQS, LEN, D), 1.0, 6.0, ((0, 4), (1, 4))),
        "segments": draw_segments(jax.random.fold_in(arg_keys[12], 71), 0),
        "cotangent": centred(arg_keys[2], (SEQS, LEN, D), 1.0, 6.0, ((0, 4), (1, 4))),
        "attn_gain": jnp.clip(0.5 + 1.0 * jax.random.uniform(arg_keys[3], (D,), jnp.float32) ** block_scale(arg_keys[3], (D,), ((0, 16),), -0.2, 0.2), 0.5, 1.5).astype(jnp.bfloat16),
        "w_query": centred(arg_keys[4], (D, D), (D // 2) ** -0.5, 0.1875, ((0, 16), (1, 2))),
        "w_key": centred(arg_keys[5], (D, D), (D // 2) ** -0.5, 0.1875, ((0, 16), (1, 2))),
        "w_value": centred(arg_keys[6], (D, D), D ** -0.5, 0.125, ((0, 16), (1, 2))),
        "w_out": centred(arg_keys[7], (D, D), (D // 16) ** -0.5, 0.5, ((0, 2), (1, 16))),
        "mlp_gain": jnp.clip(0.5 + 1.0 * jax.random.uniform(arg_keys[8], (D,), jnp.float32) ** block_scale(arg_keys[8], (D,), ((0, 16),), -0.2, 0.2), 0.5, 1.5).astype(jnp.bfloat16),
        "w_gate": centred(arg_keys[9], (D, FF), D ** -0.5, 0.125, ((0, 16), (1, 2))),
        "w_up": centred(arg_keys[10], (D, FF), D ** -0.5, 0.125, ((0, 16), (1, 2))),
        "w_down": centred(arg_keys[11], (FF, D), (FF // 4) ** -0.5, 0.125, ((0, 2), (1, 16))),
    }


NORM_EPS = 1e-05
ROPE_BASE = 130000.0

@jax.custom_vjp
def low(v):
    return lax.optimization_barrier(v.astype(jnp.bfloat16)).astype(jnp.float32)

@jax.custom_vjp
def low_back(v):
    return v

def low_keep(v):
    return (low(v), None)

def low_pass(kept, grad):
    return (grad,)

def back_keep(v):
    return (v, None)

def back_low(kept, grad):
    return (low(grad),)
low.defvjp(low_keep, low_pass)
low_back.defvjp(back_keep, back_low)

def product(left, right):
    return jnp.matmul(left, right, precision=lax.Precision.HIGHEST)

def rms_scale(values, gain):
    return values * lax.rsqrt(lax.optimization_barrier(jnp.mean(values * values, axis=-1, keepdims=True)) + NORM_EPS) * gain

def doc_positions(segment_ids):
    places = jnp.arange(segment_ids.shape[0], dtype=jnp.int32)
    before = jnp.concatenate([segment_ids[:1] - 1, segment_ids[:-1]])
    starts = jnp.where(segment_ids != before, places, jnp.zeros_like(places))
    return places - lax.cummax(starts, axis=0)

def rope_tables(positions, head_dim):
    half_dim = head_dim // 2
    frequency = ROPE_BASE ** (-jnp.arange(half_dim, dtype=jnp.float32) * 2.0 / head_dim)
    angles = positions.astype(jnp.float32)[:, None] * frequency[None, :]
    return (jnp.cos(angles)[:, None, :], jnp.sin(angles)[:, None, :])

def rotate(values, cosine, sine_part):
    half_dim = values.shape[-1] // 2
    first_half = values[..., :half_dim]
    second_half = values[..., half_dim:]
    return jnp.concatenate([first_half * cosine - second_half * sine_part, second_half * cosine + first_half * sine_part], axis=-1)

def layer(values, segment_ids, params):
    attn_gain, w_query, w_key, w_value, w_out, mlp_gain, w_gate, w_up, w_down = params
    length = values.shape[0]
    cosine, sine_part = rope_tables(doc_positions(segment_ids), HEAD_DIM)
    normed = low(rms_scale(values, attn_gain))

    def split_heads(weight):
        return product(normed, weight).reshape(length, HEADS, HEAD_DIM)
    queries = low(rotate(low_back(split_heads(w_query)), cosine, sine_part))
    keys_all = low(rotate(low_back(split_heads(w_key)), cosine, sine_part))
    head_values = low(low_back(split_heads(w_value)))
    places = jnp.arange(length, dtype=jnp.int32)
    allowed = (segment_ids[:, None] == segment_ids[None, :]) & (places[None, :] <= places[:, None])

    def one_head(operands):
        query_head, key_head, value_head = operands
        scores = low_back(product(query_head, key_head.T) * 0.125)
        scores = jnp.where(allowed, scores, -1e+30)
        weights = low(jax.nn.softmax(scores, axis=-1))
        return low(low_back(product(weights, value_head)))
    attended = lax.map(jax.checkpoint(one_head), (queries.transpose(1, 0, 2), keys_all.transpose(1, 0, 2), head_values.transpose(1, 0, 2)))
    attended = attended.transpose(1, 0, 2).reshape(length, HEADS * HEAD_DIM)
    residual = values + low_back(product(attended, w_out))
    normed_two = low(rms_scale(residual, mlp_gain))
    gate_proj = low_back(product(normed_two, w_gate))
    up_proj = low_back(product(normed_two, w_up))
    hidden = low(jax.nn.silu(gate_proj) * up_proj)
    return residual + low_back(product(hidden, w_down))

def reference(tokens, segments, cotangent, attn_gain, w_query, w_key, w_value, w_out, mlp_gain, w_gate, w_up, w_down):
    params = tuple((weight.astype(jnp.float32) for weight in (attn_gain, w_query, w_key, w_value, w_out, mlp_gain, w_gate, w_up, w_down)))

    def one_sequence(totals, sample):
        seq_tokens, seq_segments, seq_cotangent = sample
        result, pullback = jax.vjp(lambda inputs, weights: layer(inputs, seq_segments, weights), seq_tokens.astype(jnp.float32), params)
        grad_input, grad_params = pullback(seq_cotangent.astype(jnp.float32))
        totals = jax.tree.map(lambda running, gradient: running + gradient, totals, grad_params)
        return (totals, (result.astype(jnp.bfloat16), grad_input))
    initial = jax.tree.map(jnp.zeros_like, params)
    totals, (block_out, grad_tokens) = lax.scan(one_sequence, initial, (tokens, segments, cotangent))
    return (block_out, grad_tokens, totals[0], totals[1], totals[2], totals[3], totals[4], totals[5], totals[6], totals[7], totals[8])
```

```python
import functools

import jax
import jax.numpy as jnp
from jax import lax
from jax.experimental import pallas as pl
from jax.experimental.pallas import tpu as pltpu
from jax.sharding import Mesh
from jax.sharding import PartitionSpec as P

HEAD_DIM = 64
HALF = HEAD_DIM // 2
PAIR = 2 * HEAD_DIM
NORM_EPS = 1e-05
ROPE_BASE = 130000.0
MASKED = -1e30
Q_BLOCK = 256
MLP_CHUNKS = 2
BF16 = jnp.bfloat16
F32 = jnp.float32


def rms_scale(values, gain):
    return values * lax.rsqrt(jnp.mean(values * values, axis=-1, keepdims=True) + NORM_EPS) * gain


def doc_starts(segment_ids):
    places = jnp.arange(segment_ids.shape[0], dtype=jnp.int32)
    before = jnp.concatenate([segment_ids[:1] - 1, segment_ids[:-1]])
    starts = jnp.where(segment_ids != before, places, jnp.zeros_like(places))
    return lax.cummax(starts, axis=0)


def rope_tables(starts):
    places = jnp.arange(starts.shape[0], dtype=jnp.int32)
    lanes = jnp.arange(PAIR, dtype=jnp.int32)
    frequency = ROPE_BASE ** (-(lanes % HALF).astype(F32) * 2.0 / HEAD_DIM)
    angles = (places - starts).astype(F32)[:, None] * frequency[None, :]
    sign = jnp.where(lanes % HEAD_DIM < HALF, -1.0, 1.0).astype(F32)
    return jnp.cos(angles), jnp.sin(angles) * sign[None, :]


def dot(left, right, contract):
    return lax.dot_general(left, right, (contract, ((), ())), preferred_element_type=F32)


def swap_halves(values):
    lanes = lax.broadcasted_iota(jnp.int32, values.shape, 1)
    return jnp.where(
        lanes % HEAD_DIM < HALF,
        pltpu.roll(values, PAIR - HALF, 1),
        pltpu.roll(values, HALF, 1),
    )


def head_lanes(values, head):
    lanes = lax.broadcasted_iota(jnp.int32, values.shape, 1)
    return jnp.where(lanes // HEAD_DIM == head, values, 0.0)


def block_scores(query, keys, starts, row):
    scores = dot(query, keys, ((1,), (1,)))
    cols = lax.broadcasted_iota(jnp.int32, scores.shape, 1)
    rows = lax.broadcasted_iota(jnp.int32, scores.shape, 0) + row
    return jnp.where((cols >= starts) & (cols <= rows), scores, MASKED)


def attention_forward(q_ref, k_ref, v_ref, cos_ref, sin_ref, start_ref, o_ref, lse_ref, km, vm):
    length = q_ref.shape[0]
    cosine, sine = cos_ref[...], sin_ref[...]
    query = q_ref[...] * cosine + swap_halves(q_ref[...]) * sine
    query = query.astype(BF16) * jnp.asarray(0.125, BF16)
    keys = k_ref[...] * cosine + swap_halves(k_ref[...]) * sine
    for head in range(2):
        km[head] = head_lanes(keys, head).astype(BF16)
        vm[head] = head_lanes(v_ref[...], head).astype(BF16)
    for row in range(0, length, Q_BLOCK):
        end = row + Q_BLOCK
        total = jnp.zeros((Q_BLOCK, PAIR), F32)
        logs = jnp.zeros((Q_BLOCK, PAIR), F32)
        lanes = lax.broadcasted_iota(jnp.int32, (Q_BLOCK, PAIR), 1)
        for head in range(2):
            scores = block_scores(
                query[row:end], km[head, :end], start_ref[row:end, :1], row
            )
            peak = jnp.max(scores, axis=-1, keepdims=True)
            weights = jnp.exp(scores - peak)
            weight_sum = jnp.sum(weights, axis=-1, keepdims=True)
            weights = (weights * (1.0 / weight_sum)).astype(BF16)
            total = total + dot(weights, vm[head, :end], ((1,), (0,)))
            logs = jnp.where(lanes // HEAD_DIM == head, peak + jnp.log(weight_sum), logs)
        o_ref[row:end] = total.astype(BF16)
        lse_ref[row:end] = logs


def attention_backward(
    q_ref, k_ref, v_ref, do_ref, lse_ref, cos_ref, sin_ref, start_ref, d_ref, km, qm, vm, dom, dq, dk, dv
):
    part = pl.program_id(1)
    length = q_ref.shape[0]

    @pl.when(part == 0)
    def _():
        cosine, sine = cos_ref[...], sin_ref[...]
        query = q_ref[...] * cosine + swap_halves(q_ref[...]) * sine
        keys = k_ref[...] * cosine + swap_halves(k_ref[...]) * sine
        grads = do_ref[...].astype(F32)
        for head in range(2):
            km[head] = head_lanes(keys, head).astype(BF16)
            qm[head] = head_lanes(query, head).astype(BF16) * jnp.asarray(0.125, BF16)
            vm[head] = head_lanes(v_ref[...], head).astype(BF16)
            dom[head] = head_lanes(grads, head).astype(BF16)
        dk[...] = jnp.zeros_like(dk)
        dv[...] = jnp.zeros_like(dv)
        for row in range(0, length, Q_BLOCK):
            end = row + Q_BLOCK
            dq_block = jnp.zeros((Q_BLOCK, PAIR), F32)
            for head in range(2):
                scores = block_scores(
                    qm[head, row:end], km[head, :end], start_ref[row:end, :1], row
                )
                lse = lse_ref[row:end, head * HEAD_DIM : head * HEAD_DIM + 1]
                probs = jnp.exp(scores - lse)
                probs_grad = dot(dom[head, row:end], vm[head, :end], ((1,), (1,)))
                inner = jnp.sum(probs * probs_grad, axis=-1, keepdims=True)
                scores_grad = (probs * (probs_grad - inner)).astype(BF16)
                dq_block = dq_block + dot(scores_grad, km[head, :end], ((1,), (0,)))
                dk[:end] += dot(scores_grad, qm[head, row:end], ((0,), (0,)))
                dv[:end] += dot(probs.astype(BF16), dom[head, row:end], ((0,), (0,)))
            dq[row:end] = dq_block
        grad = dq[...] * 0.125
        d_ref[...] = (grad * cosine - swap_halves(grad) * sine).astype(BF16)

    @pl.when(part == 1)
    def _():
        grad = dk[...].astype(BF16).astype(F32)
        d_ref[...] = (grad * cos_ref[...] - swap_halves(grad) * sin_ref[...]).astype(BF16)

    @pl.when(part == 2)
    def _():
        d_ref[...] = dv[...].astype(BF16)


def run_attention_forward(qkv, cosine, sine, starts):
    length, pairs = qkv.shape[0], qkv.shape[1] // (3 * PAIR)
    column = lambda offset: pl.BlockSpec((length, PAIR), lambda p: (0, offset + p))
    whole = pl.BlockSpec((length, PAIR), lambda p: (0, 0))
    return pl.pallas_call(
        attention_forward,
        grid=(pairs,),
        in_specs=[column(0), column(pairs), column(2 * pairs), whole, whole, whole],
        out_specs=[column(0), column(0)],
        out_shape=[
            jax.ShapeDtypeStruct((length, pairs * PAIR), BF16),
            jax.ShapeDtypeStruct((length, pairs * PAIR), F32),
        ],
        scratch_shapes=[pltpu.VMEM((2, length, PAIR), BF16)] * 2,
        compiler_params=pltpu.CompilerParams(vmem_limit_bytes=48 * 2**20),
        name="attention_forward",
    )(qkv, qkv, qkv, cosine, sine, starts)


def run_attention_backward(qkv, grads, logs, cosine, sine, starts):
    length, pairs = qkv.shape[0], qkv.shape[1] // (3 * PAIR)
    column = lambda offset: pl.BlockSpec((length, PAIR), lambda p, part: (0, offset + p))
    whole = pl.BlockSpec((length, PAIR), lambda p, part: (0, 0))
    return pl.pallas_call(
        attention_backward,
        grid=(pairs, 3),
        in_specs=[
            column(0), column(pairs), column(2 * pairs), column(0), column(0), whole, whole, whole,
        ],
        out_specs=pl.BlockSpec((length, PAIR), lambda p, part: (0, part * pairs + p)),
        out_shape=jax.ShapeDtypeStruct((length, 3 * pairs * PAIR), BF16),
        scratch_shapes=[pltpu.VMEM((2, length, PAIR), BF16)] * 4
        + [pltpu.VMEM((length, PAIR), F32)] * 3,
        compiler_params=pltpu.CompilerParams(vmem_limit_bytes=48 * 2**20),
        name="attention_backward",
    )(qkv, qkv, qkv, grads, logs, cosine, sine, starts)


def swap(values, axis, size, step):
    return lax.ppermute(values, axis, [(i, i ^ step) for i in range(size)])


def by_index(parts, index):
    parts = list(parts)
    bit = 1
    while bit < len(parts):
        odd = (index & bit) != 0
        parts = [jnp.where(odd, parts[j ^ bit], parts[j]) for j in range(len(parts))]
        bit *= 2
    return parts


def per_device(
    sizes, tokens, segments, cotangent, attn_gain, w_query, w_key, w_value, w_out, mlp_gain, w_gate, w_up, w_down
):
    ny, nc, nx = sizes
    nq = ny * nx
    yi, core, ctx, xi = (lax.axis_index(name) for name in ("y", "core", "ctx", "tensor"))
    quarter = yi * nx + xi
    group = ("y", "tensor")
    batch, chunk, width = tokens.shape
    length = segments.shape[1]
    piece_rows = chunk // nq
    rows = w_query.shape[0]

    def pick(array, index, axis):
        return lax.dynamic_index_in_dim(array, index, axis, keepdims=False)

    def permuted(values):
        lead = values.shape[:-1]
        return values.reshape(lead + (ny, 2 * nc, rows)).swapaxes(-3, -2).reshape(lead + (width,))

    def unpermuted(values):
        lead = values.shape[:-1]
        return values.reshape(lead + (2 * nc, ny, rows)).swapaxes(-3, -2).reshape(lead + (width,))

    def pieces_in(values):
        values = permuted(values).reshape(batch, nq, piece_rows, width)
        parts = [pick(values, quarter, 1)]
        for step in range(1, ny):
            parts.append(swap(pick(values, (yi ^ step) * nx + xi, 1), "y", ny, step))
        ordered = jnp.concatenate(by_index(parts, yi), axis=0)
        return lax.all_to_all(ordered, "ctx", 0, 0, tiled=True)

    def pieces_out(piece):
        held = lax.all_to_all(piece, "ctx", 0, 0, tiled=True)
        held = held.reshape(ny, batch, piece_rows, width)
        parts = [pick(held, yi, 0)]
        for step in range(1, nq):
            parts.append(swap(pick(held, (quarter ^ step) // nx, 0), group, nq, step))
        ordered = jnp.stack(by_index(parts, quarter), axis=1)
        return unpermuted(ordered.reshape(batch, chunk, width))

    def gather_rows(piece):
        out = jnp.zeros((nc, nq, piece_rows, width), piece.dtype)
        for step in range(nq):
            part = piece if step == 0 else swap(piece, group, nq, step)
            out = lax.dynamic_update_slice(out, part[:, None], (0, quarter ^ step, 0, 0))
        return out.reshape(length, width)

    def sum_rows(partial):
        partial = partial.reshape(nc, nq, piece_rows, width)
        total = pick(partial, quarter, 1).astype(F32)
        for step in range(1, nq):
            total = total + swap(pick(partial, quarter ^ step, 1), group, nq, step).astype(F32)
        return total

    def fetch(blocks):
        parts = [blocks(yi)]
        for step in range(1, ny):
            parts.append(swap(blocks(yi ^ step), "y", ny, step))
        held = jnp.concatenate(by_index(parts, yi), axis=0)
        return lax.all_gather(held, ("core", "ctx"), axis=0, tiled=True)

    def columns(weight, index, start, count):
        share = weight.shape[1] // ny
        return lax.dynamic_slice_in_dim(weight, index * share + start, count, axis=1)

    def settle(left, right):
        half = width // 2
        other = lax.dynamic_slice_in_dim(left, (1 - core) * half, half, axis=1)
        mine = lax.dynamic_slice_in_dim(left, core * half, half, axis=1)
        away = dot(other, right, ((0,), (0,))).astype(BF16)
        came = swap(away, "core", 2, 1)
        held = (dot(mine, right, ((0,), (0,))) + came.astype(F32)).astype(BF16)
        return lax.psum_scatter(held, "ctx", scatter_dimension=0, tiled=True)

    def own_rows(summed):
        summed = summed.reshape(ny, rows, -1)
        parts = [pick(summed, yi, 0)]
        for step in range(1, ny):
            parts.append(swap(pick(summed, yi ^ step, 0), "y", ny, step))
        return by_index(parts, yi)

    gains = lax.all_gather(
        jnp.concatenate([attn_gain, mlp_gain])[None], ("core", "ctx", "y"), axis=0, tiled=True
    )
    gain_one = gains[:, :rows].reshape(width).astype(F32)
    gain_two = gains[:, rows:].reshape(width).astype(F32)

    head_cols = w_query.shape[1] // ny
    qkv_weight = fetch(
        lambda index: jnp.concatenate(
            [columns(w, index, 0, head_cols) for w in (w_query, w_key, w_value)], axis=1
        )
    )
    out_turned = w_out.T
    out_weight = fetch(lambda index: columns(out_turned, index, 0, head_cols))

    seg_parts = [segments] + [swap(segments, "y", ny, step) for step in range(1, ny)]
    all_segments = jnp.concatenate(by_index(seg_parts, yi), axis=0)
    starts = doc_starts(pick(all_segments, ctx, 0))
    cosine, sine = rope_tables(starts)
    starts = jnp.broadcast_to(starts[:, None], (length, PAIR))

    x_piece = pieces_in(tokens).astype(F32)
    normed = gather_rows(rms_scale(x_piece, gain_one).astype(BF16))
    up_piece = pieces_in(cotangent)
    upstream = gather_rows(up_piece)

    hidden_cols = w_gate.shape[1] // ny
    part_cols = hidden_cols // MLP_CHUNKS
    down_turned = w_down.T
    mlp_weights = []
    for part in range(MLP_CHUNKS):
        start = part * part_cols
        gate_up = fetch(
            lambda index: jnp.concatenate(
                [columns(w, index, start, part_cols) for w in (w_gate, w_up)], axis=1
            )
        )
        mlp_weights.append((gate_up, fetch(lambda index: columns(down_turned, index, start, part_cols))))

    qkv = dot(normed, qkv_weight, ((1,), (0,)))
    attended, logs = run_attention_forward(qkv, cosine, sine, starts)
    attn_sum = sum_rows(dot(attended, out_weight, ((1,), (1,))).astype(BF16))
    residual = x_piece + attn_sum
    normed_two = gather_rows(rms_scale(residual, gain_two).astype(BF16))

    mlp_out = None
    back_two = None
    mlp_grads = []
    for gate_up, down in mlp_weights:
        both = dot(normed_two, gate_up, ((1,), (0,)))
        gate, up = both[:, :part_cols], both[:, part_cols:]
        hidden_grad = dot(upstream, down, ((1,), (0,)))
        sigmoid = jax.nn.sigmoid(gate)
        silu = gate * sigmoid
        hidden = (silu * up).astype(BF16)
        gate_grad = hidden_grad * up * (sigmoid + silu * (1.0 - sigmoid))
        both_grad = jnp.concatenate([gate_grad, hidden_grad * silu], axis=1).astype(BF16)
        term = dot(both_grad, gate_up, ((1,), (1,)))
        back_two = term if back_two is None else back_two + term
        term = dot(hidden, down, ((1,), (1,)))
        mlp_out = term if mlp_out is None else mlp_out + term
        mlp_grads.append((settle(normed_two, both_grad), settle(upstream, hidden)))

    back_two = sum_rows(back_two.astype(BF16))
    _, norm_two_back = jax.vjp(rms_scale, residual, gain_two)
    residual_grad, gain_two_grad = norm_two_back(back_two)
    residual_grad = residual_grad + up_piece.astype(F32)
    residual_low = gather_rows(residual_grad.astype(BF16))
    attended_grad = dot(residual_low, out_weight, ((1,), (0,))).astype(BF16)
    out_grad = settle(residual_low, attended)

    qkv_grad = run_attention_backward(qkv, attended_grad, logs, cosine, sine, starts)
    back_one = sum_rows(dot(qkv_grad, qkv_weight, ((1,), (1,))).astype(BF16))
    qkv_weight_grad = settle(normed, qkv_grad)
    _, norm_one_back = jax.vjp(rms_scale, x_piece, gain_one)
    inputs_grad, gain_one_grad = norm_one_back(back_one)
    grad_tokens = pieces_out((inputs_grad + residual_grad).astype(BF16)).astype(F32)
    block_out = pieces_out((residual + sum_rows(mlp_out.astype(BF16))).astype(BF16))

    gain_grads = lax.psum(
        jnp.stack([gain_one_grad, gain_two_grad]), ("y", "core", "ctx", "tensor")
    ).reshape(2, 2 * nc * ny, rows)
    gain_grads = pick(gain_grads, (core * nc + ctx) * ny + yi, 1)

    qkv_parts = own_rows(qkv_weight_grad)
    grad_query, grad_key, grad_value = (
        jnp.concatenate(
            [p[:, i * head_cols : (i + 1) * head_cols] for p in qkv_parts], axis=1
        ).astype(F32)
        for i in range(3)
    )
    grad_out = jnp.concatenate(own_rows(out_grad), axis=1).T.astype(F32)
    gate_up_parts = [own_rows(pair[0]) for pair in mlp_grads]
    down_parts = [own_rows(pair[1]) for pair in mlp_grads]
    grad_gate, grad_up = (
        jnp.concatenate(
            [p[y][:, i * part_cols : (i + 1) * part_cols] for y in range(ny) for p in gate_up_parts],
            axis=1,
        ).astype(F32)
        for i in range(2)
    )
    grad_down = jnp.concatenate([p[y] for y in range(ny) for p in down_parts], axis=1).T.astype(F32)
    return (
        block_out,
        grad_tokens,
        gain_grads[0],
        grad_query,
        grad_key,
        grad_value,
        grad_out,
        gain_grads[1],
        grad_gate,
        grad_up,
        grad_down,
    )


def solution(mesh):
    ny, nc, nx = mesh.shape["fsdp"] // 2, mesh.shape["ctx"], mesh.shape["tensor"]
    fine = Mesh(mesh.devices.reshape(ny, 2, nc, nx), ("y", "core", "ctx", "tensor"))
    fsdp = ("y", "core")
    owner = ("y", "core", "ctx")
    token_spec = P(fsdp, "ctx", None)
    weight_specs = (
        P(owner),
        P(owner, "tensor"),
        P(owner, "tensor"),
        P(owner, "tensor"),
        P("tensor", owner),
        P(owner),
        P(owner, "tensor"),
        P(owner, "tensor"),
        P("tensor", owner),
    )
    return jax.shard_map(
        functools.partial(per_device, (ny, nc, nx)),
        mesh=fine,
        in_specs=(token_spec, P(fsdp, None), token_spec) + weight_specs,
        out_specs=(token_spec, token_spec) + weight_specs,
        check_vma=False,
    )
```

```python
import functools

import jax
import jax.numpy as jnp
from jax import lax
from jax.experimental import pallas as pl
from jax.experimental.pallas import tpu as pltpu
from jax.sharding import Mesh
from jax.sharding import PartitionSpec as P

HEAD_DIM = 64
HALF = HEAD_DIM // 2
PAIR = 2 * HEAD_DIM
NORM_EPS = 1e-05
ROPE_BASE = 130000.0
MASKED = -1e30
Q_BLOCK = 256
MLP_CHUNKS = 2
TILE = 256
VMEM = 56 * 2**20
COST = pl.CostEstimate(flops=10**12, bytes_accessed=10**6, transcendentals=0)
SHORT = pl.CostEstimate(flops=10**10, bytes_accessed=10**6, transcendentals=0)
BF16 = jnp.bfloat16
F32 = jnp.float32


def rms_scale(values, gain):
    return values * lax.rsqrt(jnp.mean(values * values, axis=-1, keepdims=True) + NORM_EPS) * gain


def doc_starts(segment_ids):
    places = jnp.arange(segment_ids.shape[0], dtype=jnp.int32)
    before = jnp.concatenate([segment_ids[:1] - 1, segment_ids[:-1]])
    starts = jnp.where(segment_ids != before, places, jnp.zeros_like(places))
    return lax.cummax(starts, axis=0)


def rope_tables(starts):
    places = jnp.arange(starts.shape[0], dtype=jnp.int32)
    lanes = jnp.arange(PAIR, dtype=jnp.int32)
    frequency = ROPE_BASE ** (-(lanes % HALF).astype(F32) * 2.0 / HEAD_DIM)
    angles = (places - starts).astype(F32)[:, None] * frequency[None, :]
    sign = jnp.where(lanes % HEAD_DIM < HALF, -1.0, 1.0).astype(F32)
    return jnp.cos(angles), jnp.sin(angles) * sign[None, :]


def dot(left, right, contract):
    return lax.dot_general(left, right, (contract, ((), ())), preferred_element_type=F32)


def swap_halves(values):
    lanes = lax.broadcasted_iota(jnp.int32, values.shape, 1)
    return jnp.where(
        lanes % HEAD_DIM < HALF,
        pltpu.roll(values, PAIR - HALF, 1),
        pltpu.roll(values, HALF, 1),
    )


def head_lanes(values, head):
    lanes = lax.broadcasted_iota(jnp.int32, values.shape, 1)
    return jnp.where(lanes // HEAD_DIM == head, values, 0.0)


def block_scores(query, keys, starts, row):
    scores = dot(query, keys, ((1,), (1,)))
    cols = lax.broadcasted_iota(jnp.int32, scores.shape, 1)
    rows = lax.broadcasted_iota(jnp.int32, scores.shape, 0) + row
    return jnp.where((cols >= starts) & (cols <= rows), scores, MASKED)


def attention_forward(q_ref, k_ref, v_ref, cos_ref, sin_ref, start_ref, o_ref, lse_ref, km, vm):
    length = q_ref.shape[0]
    cosine, sine = cos_ref[...], sin_ref[...]
    query = q_ref[...] * cosine + swap_halves(q_ref[...]) * sine
    query = query.astype(BF16) * jnp.asarray(0.125, BF16)
    keys = k_ref[...] * cosine + swap_halves(k_ref[...]) * sine
    for head in range(2):
        km[head] = head_lanes(keys, head).astype(BF16)
        vm[head] = head_lanes(v_ref[...], head).astype(BF16)
    for row in range(0, length, Q_BLOCK):
        end = row + Q_BLOCK
        total = jnp.zeros((Q_BLOCK, PAIR), F32)
        logs = jnp.zeros((Q_BLOCK, PAIR), F32)
        lanes = lax.broadcasted_iota(jnp.int32, (Q_BLOCK, PAIR), 1)
        for head in range(2):
            scores = block_scores(
                query[row:end], km[head, :end], start_ref[row:end, :1], row
            )
            peak = jnp.max(scores, axis=-1, keepdims=True)
            weights = jnp.exp(scores - peak)
            weight_sum = jnp.sum(weights, axis=-1, keepdims=True)
            weights = (weights * (1.0 / weight_sum)).astype(BF16)
            total = total + dot(weights, vm[head, :end], ((1,), (0,)))
            logs = jnp.where(lanes // HEAD_DIM == head, peak + jnp.log(weight_sum), logs)
        o_ref[row:end] = total.astype(BF16)
        lse_ref[row:end] = logs


def attention_backward(
    q_ref, k_ref, v_ref, do_ref, lse_ref, cos_ref, sin_ref, start_ref, d_ref, km, qm, vm, dom, dq, dk, dv
):
    part = pl.program_id(1)
    length = q_ref.shape[0]

    @pl.when(part == 0)
    def _():
        cosine, sine = cos_ref[...], sin_ref[...]
        query = q_ref[...] * cosine + swap_halves(q_ref[...]) * sine
        keys = k_ref[...] * cosine + swap_halves(k_ref[...]) * sine
        grads = do_ref[...].astype(F32)
        for head in range(2):
            km[head] = head_lanes(keys, head).astype(BF16)
            qm[head] = head_lanes(query, head).astype(BF16) * jnp.asarray(0.125, BF16)
            vm[head] = head_lanes(v_ref[...], head).astype(BF16)
            dom[head] = head_lanes(grads, head).astype(BF16)
        dk[...] = jnp.zeros_like(dk)
        dv[...] = jnp.zeros_like(dv)
        for row in range(0, length, Q_BLOCK):
            end = row + Q_BLOCK
            dq_block = jnp.zeros((Q_BLOCK, PAIR), F32)
            for head in range(2):
                scores = block_scores(
                    qm[head, row:end], km[head, :end], start_ref[row:end, :1], row
                )
                lse = lse_ref[row:end, head * HEAD_DIM : head * HEAD_DIM + 1]
                probs = jnp.exp(scores - lse)
                probs_grad = dot(dom[head, row:end], vm[head, :end], ((1,), (1,)))
                inner = jnp.sum(probs * probs_grad, axis=-1, keepdims=True)
                scores_grad = (probs * (probs_grad - inner)).astype(BF16)
                dq_block = dq_block + dot(scores_grad, km[head, :end], ((1,), (0,)))
                dk[:end] += dot(scores_grad, qm[head, row:end], ((0,), (0,)))
                dv[:end] += dot(probs.astype(BF16), dom[head, row:end], ((0,), (0,)))
            dq[row:end] = dq_block
        grad = dq[...] * 0.125
        d_ref[...] = (grad * cosine - swap_halves(grad) * sine).astype(BF16)

    @pl.when(part == 1)
    def _():
        grad = dk[...].astype(BF16).astype(F32)
        d_ref[...] = (grad * cos_ref[...] - swap_halves(grad) * sin_ref[...]).astype(BF16)

    @pl.when(part == 2)
    def _():
        d_ref[...] = dv[...].astype(BF16)


def run_attention_forward(qkv, cosine, sine, starts):
    length, pairs = qkv.shape[0], qkv.shape[1] // (3 * PAIR)
    column = lambda offset: pl.BlockSpec((length, PAIR), lambda p: (0, offset + p))
    whole = pl.BlockSpec((length, PAIR), lambda p: (0, 0))
    return pl.pallas_call(
        attention_forward,
        grid=(pairs,),
        in_specs=[column(0), column(pairs), column(2 * pairs), whole, whole, whole],
        out_specs=[column(0), column(0)],
        out_shape=[
            jax.ShapeDtypeStruct((length, pairs * PAIR), BF16),
            jax.ShapeDtypeStruct((length, pairs * PAIR), F32),
        ],
        scratch_shapes=[pltpu.VMEM((2, length, PAIR), BF16)] * 2,
        compiler_params=pltpu.CompilerParams(vmem_limit_bytes=VMEM),
        cost_estimate=COST,
        name="attention_forward",
    )(qkv, qkv, qkv, cosine, sine, starts)


def run_attention_backward(qkv, grads, logs, cosine, sine, starts):
    length, pairs = qkv.shape[0], qkv.shape[1] // (3 * PAIR)
    column = lambda offset: pl.BlockSpec((length, PAIR), lambda p, part: (0, offset + p))
    whole = pl.BlockSpec((length, PAIR), lambda p, part: (0, 0))
    return pl.pallas_call(
        attention_backward,
        grid=(pairs, 3),
        in_specs=[
            column(0), column(pairs), column(2 * pairs), column(0), column(0), whole, whole, whole,
        ],
        out_specs=pl.BlockSpec((length, PAIR), lambda p, part: (0, part * pairs + p)),
        out_shape=jax.ShapeDtypeStruct((length, 3 * pairs * PAIR), BF16),
        scratch_shapes=[pltpu.VMEM((2, length, PAIR), BF16)] * 4
        + [pltpu.VMEM((length, PAIR), F32)] * 3,
        compiler_params=pltpu.CompilerParams(vmem_limit_bytes=VMEM),
        cost_estimate=SHORT,
        name="attention_backward",
    )(qkv, qkv, qkv, grads, logs, cosine, sine, starts)


def add_terms(terms):
    first_half = 2 * pl.program_id(0) < pl.num_programs(0)
    total = None
    for term in terms:
        if isinstance(term, tuple):
            value = jnp.where(first_half, term[0][...].astype(F32), term[1][...].astype(F32))
        else:
            value = term[...].astype(F32)
        total = value if total is None else total + value
    return total


def take_terms(refs, kinds):
    refs, terms = list(refs), []
    for kind in kinds:
        terms.append(refs.pop(0) if kind == 1 else (refs.pop(0), refs.pop(0)))
    return terms, refs


def store(out, values, order):
    step = values.shape[1] // len(order or (0,))
    for place, source in enumerate(order or (0,)):
        out[:, place * step : (place + 1) * step] = values[
            :, source * step : (source + 1) * step
        ].astype(out.dtype)


def add_rows(kinds, order, *refs):
    terms, (out,) = take_terms(refs, kinds)
    store(out, add_terms(terms), order)


def norm_forward(kinds, order, *refs):
    terms, (gain_ref, kept_ref, normed_ref) = take_terms(refs, kinds)
    store(kept_ref, add_terms(terms), order)
    normed_ref[...] = rms_scale(kept_ref[...].astype(F32), gain_ref[...]).astype(BF16)


def norm_backward(kinds, order, *refs):
    terms, (values_ref, gain_ref, above_ref, gain_grad_ref, *outs) = take_terms(refs, kinds)
    grad = add_terms(terms)
    values = values_ref[...].astype(F32)
    scale = lax.rsqrt(jnp.mean(values * values, axis=-1, keepdims=True) + NORM_EPS)
    scaled = values * scale
    term = grad * gain_ref[...]
    mean = jnp.mean(scaled * term, axis=-1, keepdims=True)
    total = above_ref[...].astype(F32) + scale * (term - scaled * mean)

    @pl.when(pl.program_id(0) == 0)
    def _():
        gain_grad_ref[...] = jnp.zeros_like(gain_grad_ref)

    gain_grad_ref[...] += jnp.sum(grad * scaled, axis=0, keepdims=True)
    for out in outs:
        store(out, total, order)


def feed_forward(normed_ref, above_ref, gate_up_ref, down_ref, hidden_ref, grad_ref):
    length, tile = hidden_ref.shape
    for row in range(0, length, Q_BLOCK):
        at = slice(row, min(row + Q_BLOCK, length))
        normed = normed_ref[at]
        gate = dot(normed, gate_up_ref[:, :tile], ((1,), (0,)))
        up = dot(normed, gate_up_ref[:, tile:], ((1,), (0,)))
        hidden_grad = dot(above_ref[at], down_ref[...], ((1,), (0,)))
        sigmoid = 1.0 / (1.0 + jnp.exp(-gate))
        silu = gate * sigmoid
        hidden_ref[at] = (silu * up).astype(BF16)
        grad_ref[at, :tile] = (hidden_grad * up * (sigmoid + silu * (1.0 - sigmoid))).astype(BF16)
        grad_ref[at, tile:] = (hidden_grad * silu).astype(BF16)


def row_terms_specs(terms, width):
    whole = [t for t in terms if not isinstance(t, tuple)][0]
    rows = whole.size // width
    block = min(rows // 2, 64)
    steps = rows // block
    row = pl.BlockSpec((block, width), lambda i: (i, 0))
    first = pl.BlockSpec((block, width), lambda i: (jnp.minimum(i, steps // 2 - 1), 0))
    second = pl.BlockSpec((block, width), lambda i: (jnp.maximum(i - steps // 2, 0), 0))
    flat, kinds, specs = [], [], []
    for term in terms:
        parts = term if isinstance(term, tuple) else (term,)
        flat += [part.reshape(-1, width) for part in parts]
        specs += [first, second] if len(parts) == 2 else [row]
        kinds.append(len(parts))
    return rows, steps, row, flat, tuple(kinds), specs


def run_add_rows(terms, order):
    shape = terms[0].shape
    width = shape[-1]
    rows, steps, row, flat, kinds, specs = row_terms_specs(terms, width)
    out = pl.pallas_call(
        functools.partial(add_rows, kinds, order),
        grid=(steps,),
        in_specs=specs,
        out_specs=row,
        out_shape=jax.ShapeDtypeStruct((rows, width), BF16),
        compiler_params=pltpu.CompilerParams(vmem_limit_bytes=VMEM),
        name="add_rows",
    )(*flat)
    return out.reshape(shape)


def run_norm_forward(terms, gain, kept, order=None):
    shape = terms[0].shape
    width = shape[-1]
    rows, steps, row, flat, kinds, specs = row_terms_specs(terms, width)
    whole = pl.BlockSpec((1, width), lambda i: (0, 0))
    outs = pl.pallas_call(
        functools.partial(norm_forward, kinds, order),
        grid=(steps,),
        in_specs=specs + [whole],
        out_specs=[row, row],
        out_shape=[jax.ShapeDtypeStruct((rows, width), kind) for kind in (kept, BF16)],
        compiler_params=pltpu.CompilerParams(vmem_limit_bytes=VMEM),
        cost_estimate=COST,
        name="norm_forward",
    )(*flat, gain[None])
    return [out.reshape(shape) for out in outs]


def run_norm_backward(terms, values, gain, above, types, cost, order=None):
    shape = values.shape
    width = shape[-1]
    rows, steps, row, flat, kinds, specs = row_terms_specs(terms, width)
    whole = pl.BlockSpec((1, width), lambda i: (0, 0))
    grad, *outs = pl.pallas_call(
        functools.partial(norm_backward, kinds, order),
        grid=(steps,),
        in_specs=specs + [row, whole, row],
        out_specs=[whole] + [row] * len(types),
        out_shape=[jax.ShapeDtypeStruct((1, width), F32)]
        + [jax.ShapeDtypeStruct((rows, width), kind) for kind in types],
        compiler_params=pltpu.CompilerParams(vmem_limit_bytes=VMEM),
        cost_estimate=cost,
        name="norm_backward",
    )(*flat, values.reshape(rows, width), gain[None], above.reshape(rows, width))
    return grad, [out.reshape(shape) for out in outs]


def turned_product(left_ref, right_ref, out_ref):
    out_ref[...] = dot(left_ref[...], right_ref[...], ((1,), (1,))).astype(BF16)


def run_turned_product(left, right):
    (length, depth), width = left.shape, right.shape[0]
    tile = min(TILE, width)
    return pl.pallas_call(
        turned_product,
        grid=(width // tile,),
        in_specs=[
            pl.BlockSpec((length, depth), lambda j: (0, 0)),
            pl.BlockSpec((tile, depth), lambda j: (j, 0)),
        ],
        out_specs=pl.BlockSpec((length, tile), lambda j: (0, j)),
        out_shape=jax.ShapeDtypeStruct((length, width), BF16),
        compiler_params=pltpu.CompilerParams(vmem_limit_bytes=VMEM),
        cost_estimate=COST,
        name="turned_product",
    )(left, right)


def run_feed_forward(normed, above, weight, part_cols):
    length, width = normed.shape
    tile = min(TILE, part_cols)
    whole = pl.BlockSpec((length, width), lambda j: (0, 0))
    return pl.pallas_call(
        feed_forward,
        grid=(part_cols // tile,),
        in_specs=[
            whole,
            whole,
            pl.BlockSpec((width, 2 * tile), lambda j: (0, j)),
            pl.BlockSpec((width, tile), lambda j: (0, 2 * part_cols // tile + j)),
        ],
        out_specs=[
            pl.BlockSpec((length, tile), lambda j: (0, j)),
            pl.BlockSpec((length, 2 * tile), lambda j: (0, j)),
        ],
        out_shape=[
            jax.ShapeDtypeStruct((length, part_cols), BF16),
            jax.ShapeDtypeStruct((length, 2 * part_cols), BF16),
        ],
        compiler_params=pltpu.CompilerParams(vmem_limit_bytes=VMEM),
        cost_estimate=COST,
        name="feed_forward",
    )(normed, above, weight, weight)


def swap(values, axis, size, step):
    return lax.ppermute(values, axis, [(i, i ^ step) for i in range(size)])


def after(values, *others):
    return lax.optimization_barrier((values,) + others)[0]


def by_index(parts, index):
    parts = list(parts)
    bit = 1
    while bit < len(parts):
        odd = (index & bit) != 0
        parts = [jnp.where(odd, parts[j ^ bit], parts[j]) for j in range(len(parts))]
        bit *= 2
    return parts


def per_device(
    sizes, tokens, segments, cotangent, attn_gain, w_query, w_key, w_value, w_out, mlp_gain, w_gate, w_up, w_down
):
    ny, nc, nx = sizes
    nq = ny * nx
    yi, core, ctx, xi = (lax.axis_index(name) for name in ("y", "core", "ctx", "tensor"))
    quarter = yi * nx + xi
    group = ("y", "tensor")
    batch, chunk, width = tokens.shape
    length = segments.shape[1]
    piece_rows = chunk // nq
    rows = w_query.shape[0]
    half = width // 2

    def pick(array, index, axis):
        return lax.dynamic_index_in_dim(array, index, axis, keepdims=False)

    inward = tuple(y * 2 * nc + k for k in range(2 * nc) for y in range(ny))
    outward = tuple(k * ny + y for y in range(ny) for k in range(2 * nc))

    def over_y(blocks):
        parts = [blocks(yi)]
        for step in range(1, ny):
            parts.append(swap(blocks(yi ^ step), "y", ny, step))
        return by_index(parts, yi)

    def rows_for(values):
        values = values.reshape(batch, nq, piece_rows, width)
        return jnp.concatenate(over_y(lambda index: pick(values, index * nx + xi, 1)), axis=0)

    def turn(pieces):
        return lax.all_to_all(pieces, "ctx", 0, 0, tiled=True)

    def pieces_out(held):
        held = held.reshape(ny, batch, piece_rows, width)
        parts = [pick(held, yi, 0)]
        for step in range(1, nq):
            parts.append(swap(pick(held, (quarter ^ step) // nx, 0), group, nq, step))
        ordered = jnp.stack(by_index(parts, quarter), axis=1)
        return ordered.reshape(batch, chunk, width)

    corner = nq == 4 and nx == 2 and nc % 2 == 0
    cut = nc // 2

    def gather_rows(piece):
        out = jnp.zeros((nc, nq, piece_rows, width), piece.dtype)

        def put(out, part, step, start=0):
            return lax.dynamic_update_slice(out, part[:, None], (start, quarter ^ step, 0, 0))

        if not corner:
            for step in range(nq):
                out = put(out, piece if step == 0 else swap(piece, group, nq, step), step)
            return out.reshape(length, width)
        by_x, by_y = swap(piece, group, nq, 1), swap(piece, group, nq, 2)
        far_x, far_y = swap(by_y[:cut], group, nq, 1), swap(by_x[cut:], group, nq, 2)
        out = put(put(put(out, piece, 0), by_x, 1), by_y, 2)
        return put(put(out, far_x, 3), far_y, 3, cut).reshape(length, width)

    def row_terms(partial, *beside):
        partial = partial.reshape(nc, nq, piece_rows, width)

        def term(step):
            return pick(partial, quarter ^ step, 1)

        if not corner:
            return [term(0)] + [swap(term(step), group, nq, step) for step in range(1, nq)]
        far, to_x, to_y = term(3), term(1), term(2)
        from_x, from_y = swap(far[:cut], group, nq, 1), swap(far[cut:], group, nq, 2)
        x_first, y_last = swap(to_x[:cut], group, nq, 1), swap(to_y[cut:], group, nq, 2)
        to_x, to_y = after(to_x[cut:], *beside), after(to_y[:cut], *beside)
        to_x = (to_x.astype(F32) + from_y.astype(F32)).astype(BF16)
        to_y = (to_y.astype(F32) + from_x.astype(F32)).astype(BF16)
        return [
            term(0),
            (x_first, swap(to_x, group, nq, 1)),
            (swap(to_y, group, nq, 2), y_last),
        ]

    def fetch(held):
        return lax.all_gather(held, ("core", "ctx"), axis=0, tiled=True)

    def columns(weight, index, start, count):
        share = weight.shape[1] // ny
        return lax.dynamic_slice_in_dim(weight, index * share + start, count, axis=1)

    def core_half(values, index):
        return lax.dynamic_slice_in_dim(values, index * half, half, axis=1)

    def partials(left, right, dim):
        def term(index):
            pair = (core_half(left, index), right) if dim == 0 else (left, core_half(right, index))
            return dot(*pair, ((0,), (0,)))

        came = swap(term(1 - core).astype(BF16), "core", 2, 1)
        return (term(core) + came.astype(F32)).astype(BF16)

    def settle(held, dim):
        return lax.psum_scatter(held, "ctx", scatter_dimension=dim, tiled=True)

    def own_rows(summed, dim):
        return over_y(lambda index: lax.dynamic_slice_in_dim(summed, index * rows, rows, axis=dim))

    def gain_settle(grads):
        def add(values, axis, size):
            return sum((swap(values, axis, size, step) for step in range(1, size)), values)

        grads = add(add(add(grads, group, nq), "core", 2), "ctx", nc)
        return pick(grads.reshape(2, 2 * nc * ny, rows), (core * nc + ctx) * ny + yi, 1)

    head_cols = w_query.shape[1] // ny
    hidden_cols = w_gate.shape[1] // ny
    part_cols = hidden_cols // MLP_CHUNKS
    out_turned, down_turned = w_out.T, w_down.T
    wanted = [[(w, 0, head_cols) for w in (w_query, w_key, w_value, out_turned)]]
    tile = min(TILE, part_cols)
    tiles = part_cols // tile
    for part in range(MLP_CHUNKS):
        start = part * part_cols
        wanted.append(
            [(w, start + i * tile, tile) for i in range(tiles) for w in (w_gate, w_up)]
            + [(down_turned, start, part_cols)]
        )

    def prepare(sources, *before):
        def block(index):
            return after(jnp.concatenate([columns(w, index, *p) for w, *p in sources], axis=1), *before)

        return jnp.concatenate(over_y(block), axis=0)

    x_rows = rows_for(tokens)
    x_low = turn(x_rows)
    held = prepare(wanted[0])
    weights = [fetch(after(held, x_rows))]
    for sources in wanted[1:]:
        held = prepare(sources, held, x_rows)
        weights.append(fetch(held))
    qkv_weight, out_weight = weights[0][:, : 3 * head_cols], weights[0][:, 3 * head_cols :]

    gains = jnp.concatenate([attn_gain, mlp_gain])[None]
    for axis, size, index in (("y", ny, yi), ("ctx", nc, ctx), ("core", 2, core)):
        step = 1
        while step < size:
            other = swap(gains, axis, size, step)
            odd = (index & step) != 0
            gains = jnp.concatenate([jnp.where(odd, other, gains), jnp.where(odd, gains, other)])
            step *= 2
    gain_one = gains[:, :rows].reshape(width).astype(F32)
    gain_two = gains[:, rows:].reshape(width).astype(F32)

    seg_parts = [segments] + [swap(segments, "y", ny, step) for step in range(1, ny)]
    all_segments = jnp.concatenate(by_index(seg_parts, yi), axis=0)
    starts = doc_starts(pick(all_segments, ctx, 0))
    cosine, sine = rope_tables(starts)
    starts = jnp.broadcast_to(starts[:, None], (length, PAIR))

    x_low, normed_piece = run_norm_forward([x_low], gain_one, BF16, inward)
    normed = gather_rows(normed_piece)
    up_piece = run_add_rows([turn(rows_for(after(cotangent, x_low)))], inward)
    upstream = gather_rows(after(up_piece, normed))

    qkv = dot(normed, qkv_weight, ((1,), (0,)))
    attended, logs = run_attention_forward(qkv, cosine, sine, starts)
    attn_terms = row_terms(dot(attended, out_weight, ((1,), (1,))).astype(BF16))
    residual, normed_two = run_norm_forward([x_low] + attn_terms, gain_two, F32)
    normed_two = gather_rows(normed_two)

    mlp_out = None
    back_two = None
    mlp_sums = []
    wait_for = []
    now_two = normed_two
    for part in range(MLP_CHUNKS):
        weight = weights[1 + part]
        gate_up, down = weight[:, : 2 * part_cols], weight[:, 2 * part_cols :]
        hidden, both_grad = run_feed_forward(now_two, upstream, weight, part_cols)
        term = dot(both_grad, gate_up, ((1,), (1,)))
        back_two = term if back_two is None else back_two + term
        if part + 1 == MLP_CHUNKS:
            back_two = back_two.astype(BF16)
            hidden, both_grad = after(hidden, back_two), after(both_grad, back_two)
        held_both, held_down = partials(normed_two, both_grad, 0), partials(hidden, upstream, 1)
        sums = [(settle(held_down, 1), 1), (settle(held_both, 0), 0)]
        if part + 1 < MLP_CHUNKS:
            now_two = after(now_two, held_both, held_down)
            wait_for += [summed for summed, _ in sums]
        mlp_sums.append(sums)
        term = dot(hidden, down, ((1,), (1,)))
        mlp_out = term if mlp_out is None else mlp_out + term

    mlp_out = mlp_out.astype(BF16)
    back_terms = row_terms(back_two, held_both, held_down, mlp_out)
    back_terms[0] = after(back_terms[0], *wait_for)
    gain_two_grad, (residual_grad, residual_low) = run_norm_backward(
        back_terms, residual, gain_two, up_piece, [F32, BF16], COST
    )
    residual_low = gather_rows(residual_low)
    attended_grad = dot(residual_low, out_weight, ((1,), (0,))).astype(BF16)
    qkv_grad = run_attention_backward(qkv, attended_grad, logs, cosine, sine, starts)
    attn_held = jnp.concatenate(
        [partials(normed, qkv_grad, 0), partials(residual_low, after(attended, attended_grad), 0)], axis=1
    )
    attn_summed = settle(attn_held, 0)
    back_one = run_turned_product(after(qkv_grad, attn_held, *[t for t, _ in mlp_sums[-1]]), weights[0])
    one_terms = row_terms(back_one)
    mlp_terms = row_terms(after(mlp_out, residual_low), attn_held)
    block_out = turn(run_add_rows([after(residual, back_one)] + mlp_terms, outward))
    gain_one_grad, (inputs_grad,) = run_norm_backward(
        one_terms, x_low, gain_one, residual_grad, [BF16], SHORT, outward
    )
    block_out = pieces_out(after(block_out, inputs_grad))
    grad_tokens = pieces_out(turn(inputs_grad)).astype(F32)
    gain_grads = gain_settle(jnp.concatenate([gain_one_grad, gain_two_grad]))
    mlp_grads = [
        [
            own_rows(after(summed, back_one if part + 1 < MLP_CHUNKS else inputs_grad), dim)
            for summed, dim in pair
        ]
        for part, pair in enumerate(mlp_sums)
    ]
    attn_grads = own_rows(attn_summed, 0)

    grad_query, grad_key, grad_value = (
        jnp.concatenate(
            [p[:, i * head_cols : (i + 1) * head_cols] for p in attn_grads], axis=1
        ).astype(F32)
        for i in range(3)
    )
    grad_out = jnp.concatenate([p[:, 3 * head_cols :] for p in attn_grads], axis=1).T.astype(F32)
    grad_gate, grad_up = (
        jnp.concatenate(
            [
                pair[-1][y][:, (2 * j + i) * tile : (2 * j + i + 1) * tile]
                for y in range(ny)
                for pair in mlp_grads
                for j in range(tiles)
            ],
            axis=1,
        ).astype(F32)
        for i in range(2)
    )
    grad_down = jnp.concatenate(
        [pair[0][y] for y in range(ny) for pair in mlp_grads], axis=0
    ).astype(F32)
    return (
        block_out,
        grad_tokens,
        gain_grads[0],
        grad_query,
        grad_key,
        grad_value,
        grad_out,
        gain_grads[1],
        grad_gate,
        grad_up,
        grad_down,
    )


def solution(mesh):
    ny, nc, nx = mesh.shape["fsdp"] // 2, mesh.shape["ctx"], mesh.shape["tensor"]
    fine = Mesh(mesh.devices.reshape(ny, 2, nc, nx), ("y", "core", "ctx", "tensor"))
    fsdp = ("y", "core")
    owner = ("y", "core", "ctx")
    token_spec = P(fsdp, "ctx", None)
    weight_specs = (
        P(owner),
        P(owner, "tensor"),
        P(owner, "tensor"),
        P(owner, "tensor"),
        P("tensor", owner),
        P(owner),
        P(owner, "tensor"),
        P(owner, "tensor"),
        P("tensor", owner),
    )
    return jax.shard_map(
        functools.partial(per_device, (ny, nc, nx)),
        mesh=fine,
        in_specs=(token_spec, P(fsdp, None), token_spec) + weight_specs,
        out_specs=(token_spec, token_spec) + weight_specs,
        check_vma=False,
    )
```

```python
import functools

import jax
import jax.numpy as jnp
from jax import lax
from jax.experimental import pallas as pl
from jax.experimental.pallas import tpu as pltpu
from jax.sharding import Mesh
from jax.sharding import PartitionSpec as P

HEAD_DIM = 64
HALF = HEAD_DIM // 2
PAIR = 2 * HEAD_DIM
NORM_EPS = 1e-05
ROPE_BASE = 130000.0
MASKED = -1e30
Q_BLOCK = 256
MLP_CHUNKS = 2
TILE = 256
VMEM = 56 * 2**20
COST = pl.CostEstimate(flops=10**12, bytes_accessed=10**6, transcendentals=0)
SHORT = pl.CostEstimate(flops=10**10, bytes_accessed=10**6, transcendentals=0)
BF16 = jnp.bfloat16
F32 = jnp.float32


def rms_scale(values, gain):
    return values * lax.rsqrt(jnp.mean(values * values, axis=-1, keepdims=True) + NORM_EPS) * gain


def doc_starts(segment_ids):
    places = jnp.arange(segment_ids.shape[0], dtype=jnp.int32)
    before = jnp.concatenate([segment_ids[:1] - 1, segment_ids[:-1]])
    starts = jnp.where(segment_ids != before, places, jnp.zeros_like(places))
    return lax.cummax(starts, axis=0)


def rope_tables(starts):
    places = jnp.arange(starts.shape[0], dtype=jnp.int32)
    lanes = jnp.arange(PAIR, dtype=jnp.int32)
    frequency = ROPE_BASE ** (-(lanes % HALF).astype(F32) * 2.0 / HEAD_DIM)
    angles = (places - starts).astype(F32)[:, None] * frequency[None, :]
    sign = jnp.where(lanes % HEAD_DIM < HALF, -1.0, 1.0).astype(F32)
    return jnp.cos(angles), jnp.sin(angles) * sign[None, :]


def dot(left, right, contract):
    return lax.dot_general(left, right, (contract, ((), ())), preferred_element_type=F32)


def swap_halves(values):
    lanes = lax.broadcasted_iota(jnp.int32, values.shape, 1)
    return jnp.where(
        lanes % HEAD_DIM < HALF,
        pltpu.roll(values, PAIR - HALF, 1),
        pltpu.roll(values, HALF, 1),
    )


def head_lanes(values, head):
    lanes = lax.broadcasted_iota(jnp.int32, values.shape, 1)
    return jnp.where(lanes // HEAD_DIM == head, values, 0.0)


def block_scores(query, keys, starts, row):
    scores = dot(query, keys, ((1,), (1,)))
    cols = lax.broadcasted_iota(jnp.int32, scores.shape, 1)
    rows = lax.broadcasted_iota(jnp.int32, scores.shape, 0) + row
    return jnp.where((cols >= starts) & (cols <= rows), scores, MASKED)


def attention_forward(q_ref, k_ref, v_ref, cos_ref, sin_ref, start_ref, o_ref, lse_ref, km, vm):
    length = q_ref.shape[0]
    cosine, sine = cos_ref[...], sin_ref[...]
    query = q_ref[...] * cosine + swap_halves(q_ref[...]) * sine
    query = query.astype(BF16) * jnp.asarray(0.125, BF16)
    keys = k_ref[...] * cosine + swap_halves(k_ref[...]) * sine
    for head in range(2):
        km[head] = head_lanes(keys, head).astype(BF16)
        vm[head] = head_lanes(v_ref[...], head).astype(BF16)
    for row in range(0, length, Q_BLOCK):
        end = row + Q_BLOCK
        total = jnp.zeros((Q_BLOCK, PAIR), F32)
        logs = jnp.zeros((Q_BLOCK, PAIR), F32)
        lanes = lax.broadcasted_iota(jnp.int32, (Q_BLOCK, PAIR), 1)
        for head in range(2):
            scores = block_scores(
                query[row:end], km[head, :end], start_ref[row:end, :1], row
            )
            peak = jnp.max(scores, axis=-1, keepdims=True)
            weights = jnp.exp(scores - peak)
            weight_sum = jnp.sum(weights, axis=-1, keepdims=True)
            weights = (weights * (1.0 / weight_sum)).astype(BF16)
            total = total + dot(weights, vm[head, :end], ((1,), (0,)))
            logs = jnp.where(lanes // HEAD_DIM == head, peak + jnp.log(weight_sum), logs)
        o_ref[row:end] = total.astype(BF16)
        lse_ref[row:end] = logs


def attention_backward(
    q_ref, k_ref, v_ref, do_ref, lse_ref, cos_ref, sin_ref, start_ref, d_ref, km, qm, vm, dom, dq, dk, dv
):
    part = pl.program_id(1)
    length = q_ref.shape[0]

    @pl.when(part == 0)
    def _():
        cosine, sine = cos_ref[...], sin_ref[...]
        query = q_ref[...] * cosine + swap_halves(q_ref[...]) * sine
        keys = k_ref[...] * cosine + swap_halves(k_ref[...]) * sine
        grads = do_ref[...].astype(F32)
        for head in range(2):
            km[head] = head_lanes(keys, head).astype(BF16)
            qm[head] = head_lanes(query, head).astype(BF16) * jnp.asarray(0.125, BF16)
            vm[head] = head_lanes(v_ref[...], head).astype(BF16)
            dom[head] = head_lanes(grads, head).astype(BF16)
        dk[...] = jnp.zeros_like(dk)
        dv[...] = jnp.zeros_like(dv)
        for row in range(0, length, Q_BLOCK):
            end = row + Q_BLOCK
            dq_block = jnp.zeros((Q_BLOCK, PAIR), F32)
            for head in range(2):
                scores = block_scores(
                    qm[head, row:end], km[head, :end], start_ref[row:end, :1], row
                )
                lse = lse_ref[row:end, head * HEAD_DIM : head * HEAD_DIM + 1]
                probs = jnp.exp(scores - lse)
                probs_grad = dot(dom[head, row:end], vm[head, :end], ((1,), (1,)))
                inner = jnp.sum(probs * probs_grad, axis=-1, keepdims=True)
                scores_grad = (probs * (probs_grad - inner)).astype(BF16)
                dq_block = dq_block + dot(scores_grad, km[head, :end], ((1,), (0,)))
                dk[:end] += dot(scores_grad, qm[head, row:end], ((0,), (0,)))
                dv[:end] += dot(probs.astype(BF16), dom[head, row:end], ((0,), (0,)))
            dq[row:end] = dq_block
        grad = dq[...] * 0.125
        d_ref[...] = (grad * cosine - swap_halves(grad) * sine).astype(BF16)

    @pl.when(part == 1)
    def _():
        grad = dk[...].astype(BF16).astype(F32)
        d_ref[...] = (grad * cos_ref[...] - swap_halves(grad) * sin_ref[...]).astype(BF16)

    @pl.when(part == 2)
    def _():
        d_ref[...] = dv[...].astype(BF16)


def run_attention_forward(qkv, cosine, sine, starts):
    length, pairs = qkv.shape[0], qkv.shape[1] // (3 * PAIR)
    column = lambda offset: pl.BlockSpec((length, PAIR), lambda p: (0, offset + p))
    whole = pl.BlockSpec((length, PAIR), lambda p: (0, 0))
    return pl.pallas_call(
        attention_forward,
        grid=(pairs,),
        in_specs=[column(0), column(pairs), column(2 * pairs), whole, whole, whole],
        out_specs=[column(0), column(0)],
        out_shape=[
            jax.ShapeDtypeStruct((length, pairs * PAIR), BF16),
            jax.ShapeDtypeStruct((length, pairs * PAIR), F32),
        ],
        scratch_shapes=[pltpu.VMEM((2, length, PAIR), BF16)] * 2,
        compiler_params=pltpu.CompilerParams(vmem_limit_bytes=VMEM),
        cost_estimate=COST,
        name="attention_forward",
    )(qkv, qkv, qkv, cosine, sine, starts)


def run_attention_backward(qkv, grads, logs, cosine, sine, starts):
    length, pairs = qkv.shape[0], qkv.shape[1] // (3 * PAIR)
    column = lambda offset: pl.BlockSpec((length, PAIR), lambda p, part: (0, offset + p))
    whole = pl.BlockSpec((length, PAIR), lambda p, part: (0, 0))
    return pl.pallas_call(
        attention_backward,
        grid=(pairs, 3),
        in_specs=[
            column(0), column(pairs), column(2 * pairs), column(0), column(0), whole, whole, whole,
        ],
        out_specs=pl.BlockSpec((length, PAIR), lambda p, part: (0, part * pairs + p)),
        out_shape=jax.ShapeDtypeStruct((length, 3 * pairs * PAIR), BF16),
        scratch_shapes=[pltpu.VMEM((2, length, PAIR), BF16)] * 4
        + [pltpu.VMEM((length, PAIR), F32)] * 3,
        compiler_params=pltpu.CompilerParams(vmem_limit_bytes=VMEM),
        cost_estimate=SHORT,
        name="attention_backward",
    )(qkv, qkv, qkv, grads, logs, cosine, sine, starts)


def add_terms(terms):
    first_half = 2 * pl.program_id(0) < pl.num_programs(0)
    total = None
    for term in terms:
        if isinstance(term, tuple):
            value = jnp.where(first_half, term[0][...].astype(F32), term[1][...].astype(F32))
        else:
            value = term[...].astype(F32)
        total = value if total is None else total + value
    return total


def take_terms(refs, kinds):
    refs, terms = list(refs), []
    for kind in kinds:
        terms.append(refs.pop(0) if kind == 1 else (refs.pop(0), refs.pop(0)))
    return terms, refs


def store(out, values, order):
    step = values.shape[1] // len(order or (0,))
    for place, source in enumerate(order or (0,)):
        out[:, place * step : (place + 1) * step] = values[
            :, source * step : (source + 1) * step
        ].astype(out.dtype)


def add_rows(kinds, order, *refs):
    terms, (out,) = take_terms(refs, kinds)
    store(out, add_terms(terms), order)


def norm_forward(kinds, order, *refs):
    terms, (gain_ref, kept_ref, normed_ref) = take_terms(refs, kinds)
    store(kept_ref, add_terms(terms), order)
    normed_ref[...] = rms_scale(kept_ref[...].astype(F32), gain_ref[...]).astype(BF16)


def norm_backward(kinds, order, *refs):
    terms, (values_ref, gain_ref, above_ref, gain_grad_ref, *outs) = take_terms(refs, kinds)
    grad = add_terms(terms)
    values = values_ref[...].astype(F32)
    scale = lax.rsqrt(jnp.mean(values * values, axis=-1, keepdims=True) + NORM_EPS)
    scaled = values * scale
    term = grad * gain_ref[...]
    mean = jnp.mean(scaled * term, axis=-1, keepdims=True)
    total = above_ref[...].astype(F32) + scale * (term - scaled * mean)

    @pl.when(pl.program_id(0) == 0)
    def _():
        gain_grad_ref[...] = jnp.zeros_like(gain_grad_ref)

    gain_grad_ref[...] += jnp.sum(grad * scaled, axis=0, keepdims=True)
    for out in outs:
        store(out, total, order)


def feed_forward(normed_ref, above_ref, gate_up_ref, down_ref, hidden_ref, grad_ref):
    length, tile = hidden_ref.shape
    for row in range(0, length, Q_BLOCK):
        at = slice(row, min(row + Q_BLOCK, length))
        normed = normed_ref[at]
        gate = dot(normed, gate_up_ref[:, :tile], ((1,), (0,)))
        up = dot(normed, gate_up_ref[:, tile:], ((1,), (0,)))
        hidden_grad = dot(above_ref[at], down_ref[...], ((1,), (0,)))
        sigmoid = 1.0 / (1.0 + jnp.exp(-gate))
        silu = gate * sigmoid
        hidden_ref[at] = (silu * up).astype(BF16)
        grad_ref[at, :tile] = (hidden_grad * up * (sigmoid + silu * (1.0 - sigmoid))).astype(BF16)
        grad_ref[at, tile:] = (hidden_grad * silu).astype(BF16)


def row_terms_specs(terms, width):
    whole = [t for t in terms if not isinstance(t, tuple)][0]
    rows = whole.size // width
    block = min(rows // 2, 64)
    steps = rows // block
    row = pl.BlockSpec((block, width), lambda i: (i, 0))
    first = pl.BlockSpec((block, width), lambda i: (jnp.minimum(i, steps // 2 - 1), 0))
    second = pl.BlockSpec((block, width), lambda i: (jnp.maximum(i - steps // 2, 0), 0))
    flat, kinds, specs = [], [], []
    for term in terms:
        parts = term if isinstance(term, tuple) else (term,)
        flat += [part.reshape(-1, width) for part in parts]
        specs += [first, second] if len(parts) == 2 else [row]
        kinds.append(len(parts))
    return rows, steps, row, flat, tuple(kinds), specs


def run_add_rows(terms, order):
    shape = terms[0].shape
    width = shape[-1]
    rows, steps, row, flat, kinds, specs = row_terms_specs(terms, width)
    out = pl.pallas_call(
        functools.partial(add_rows, kinds, order),
        grid=(steps,),
        in_specs=specs,
        out_specs=row,
        out_shape=jax.ShapeDtypeStruct((rows, width), BF16),
        compiler_params=pltpu.CompilerParams(vmem_limit_bytes=VMEM),
        name="add_rows",
    )(*flat)
    return out.reshape(shape)


def run_norm_forward(terms, gain, kept, order=None):
    shape = terms[0].shape
    width = shape[-1]
    rows, steps, row, flat, kinds, specs = row_terms_specs(terms, width)
    whole = pl.BlockSpec((1, width), lambda i: (0, 0))
    outs = pl.pallas_call(
        functools.partial(norm_forward, kinds, order),
        grid=(steps,),
        in_specs=specs + [whole],
        out_specs=[row, row],
        out_shape=[jax.ShapeDtypeStruct((rows, width), kind) for kind in (kept, BF16)],
        compiler_params=pltpu.CompilerParams(vmem_limit_bytes=VMEM),
        cost_estimate=COST,
        name="norm_forward",
    )(*flat, gain[None])
    return [out.reshape(shape) for out in outs]


def run_norm_backward(terms, values, gain, above, types, cost, order=None):
    shape = values.shape
    width = shape[-1]
    rows, steps, row, flat, kinds, specs = row_terms_specs(terms, width)
    whole = pl.BlockSpec((1, width), lambda i: (0, 0))
    grad, *outs = pl.pallas_call(
        functools.partial(norm_backward, kinds, order),
        grid=(steps,),
        in_specs=specs + [row, whole, row],
        out_specs=[whole] + [row] * len(types),
        out_shape=[jax.ShapeDtypeStruct((1, width), F32)]
        + [jax.ShapeDtypeStruct((rows, width), kind) for kind in types],
        compiler_params=pltpu.CompilerParams(vmem_limit_bytes=VMEM),
        cost_estimate=cost,
        name="norm_backward",
    )(*flat, values.reshape(rows, width), gain[None], above.reshape(rows, width))
    return grad, [out.reshape(shape) for out in outs]


def turned_product(left_ref, right_ref, out_ref):
    out_ref[...] = dot(left_ref[...], right_ref[...], ((1,), (1,))).astype(BF16)


def run_turned_product(left, right):
    (length, depth), width = left.shape, right.shape[0]
    tile = min(TILE, width)
    return pl.pallas_call(
        turned_product,
        grid=(width // tile,),
        in_specs=[
            pl.BlockSpec((length, depth), lambda j: (0, 0)),
            pl.BlockSpec((tile, depth), lambda j: (j, 0)),
        ],
        out_specs=pl.BlockSpec((length, tile), lambda j: (0, j)),
        out_shape=jax.ShapeDtypeStruct((length, width), BF16),
        compiler_params=pltpu.CompilerParams(vmem_limit_bytes=VMEM),
        cost_estimate=COST,
        name="turned_product",
    )(left, right)


def run_feed_forward(normed, above, weight, part_cols):
    length, width = normed.shape
    tile = min(TILE, part_cols)
    whole = pl.BlockSpec((length, width), lambda j: (0, 0))
    return pl.pallas_call(
        feed_forward,
        grid=(part_cols // tile,),
        in_specs=[
            whole,
            whole,
            pl.BlockSpec((width, 2 * tile), lambda j: (0, j)),
            pl.BlockSpec((width, tile), lambda j: (0, 2 * part_cols // tile + j)),
        ],
        out_specs=[
            pl.BlockSpec((length, tile), lambda j: (0, j)),
            pl.BlockSpec((length, 2 * tile), lambda j: (0, j)),
        ],
        out_shape=[
            jax.ShapeDtypeStruct((length, part_cols), BF16),
            jax.ShapeDtypeStruct((length, 2 * part_cols), BF16),
        ],
        compiler_params=pltpu.CompilerParams(vmem_limit_bytes=VMEM),
        cost_estimate=COST,
        name="feed_forward",
    )(normed, above, weight, weight)


def swap(values, axis, size, step):
    return lax.ppermute(values, axis, [(i, i ^ step) for i in range(size)])


def after(values, *others):
    return lax.optimization_barrier((values,) + others)[0] if others else values


def by_index(parts, index):
    parts = list(parts)
    bit = 1
    while bit < len(parts):
        odd = (index & bit) != 0
        parts = [jnp.where(odd, parts[j ^ bit], parts[j]) for j in range(len(parts))]
        bit *= 2
    return parts


def per_device(
    sizes, tokens, segments, cotangent, attn_gain, w_query, w_key, w_value, w_out, mlp_gain, w_gate, w_up, w_down
):
    ny, nc, nx = sizes
    nq = ny * nx
    yi, core, ctx, xi = (lax.axis_index(name) for name in ("y", "core", "ctx", "tensor"))
    quarter = yi * nx + xi
    group = ("y", "tensor")
    batch, chunk, width = tokens.shape
    length = segments.shape[1]
    piece_rows = chunk // nq
    rows = w_query.shape[0]
    half = width // 2

    def pick(array, index, axis):
        return lax.dynamic_index_in_dim(array, index, axis, keepdims=False)

    inward = tuple(y * 2 * nc + k for k in range(2 * nc) for y in range(ny))
    outward = tuple(k * ny + y for y in range(ny) for k in range(2 * nc))

    def over_y(blocks):
        parts = [blocks(yi)]
        for step in range(1, ny):
            parts.append(swap(blocks(yi ^ step), "y", ny, step))
        return by_index(parts, yi)

    def rows_for(values):
        values = values.reshape(batch, nq, piece_rows, width)
        return jnp.concatenate(over_y(lambda index: pick(values, index * nx + xi, 1)), axis=0)

    def turn(pieces):
        return lax.all_to_all(pieces, "ctx", 0, 0, tiled=True)

    def pieces_out(held):
        held = held.reshape(ny, batch, piece_rows, width)
        parts = [pick(held, yi, 0)]
        for step in range(1, nq):
            parts.append(swap(pick(held, (quarter ^ step) // nx, 0), group, nq, step))
        ordered = jnp.stack(by_index(parts, quarter), axis=1)
        return ordered.reshape(batch, chunk, width)

    corner = nq == 4 and nx == 2 and nc % 2 == 0
    cut = nc // 2

    def gather_rows(piece):
        out = jnp.zeros((nc, nq, piece_rows, width), piece.dtype)

        def put(out, part, step, start=0):
            return lax.dynamic_update_slice(out, part[:, None], (start, quarter ^ step, 0, 0))

        if not corner:
            for step in range(nq):
                out = put(out, piece if step == 0 else swap(piece, group, nq, step), step)
            return out.reshape(length, width)
        by_x, by_y = swap(piece, group, nq, 1), swap(piece, group, nq, 2)
        far_x, far_y = swap(by_y[:cut], group, nq, 1), swap(by_x[cut:], group, nq, 2)
        out = put(put(put(out, piece, 0), by_x, 1), by_y, 2)
        return put(put(out, far_x, 3), far_y, 3, cut).reshape(length, width)

    def row_terms(partial, *beside):
        partial = partial.reshape(nc, nq, piece_rows, width)

        def term(step):
            return pick(partial, quarter ^ step, 1)

        if not corner:
            return [term(0)] + [swap(term(step), group, nq, step) for step in range(1, nq)]
        far, to_x, to_y = term(3), term(1), term(2)
        from_x, from_y = swap(far[:cut], group, nq, 1), swap(far[cut:], group, nq, 2)
        x_first, y_last = swap(to_x[:cut], group, nq, 1), swap(to_y[cut:], group, nq, 2)
        to_x, to_y = after(to_x[cut:], *beside), after(to_y[:cut], *beside)
        to_x = (to_x.astype(F32) + from_y.astype(F32)).astype(BF16)
        to_y = (to_y.astype(F32) + from_x.astype(F32)).astype(BF16)
        return [
            term(0),
            (x_first, swap(to_x, group, nq, 1)),
            (swap(to_y, group, nq, 2), y_last),
        ]

    def fetch(held):
        return lax.all_gather(held, ("core", "ctx"), axis=0, tiled=True)

    def columns(weight, index, start, count):
        share = weight.shape[1] // ny
        return lax.dynamic_slice_in_dim(weight, index * share + start, count, axis=1)

    def core_half(values, index):
        return lax.dynamic_slice_in_dim(values, index * half, half, axis=1)

    def partials(left, right, dim):
        def term(index):
            pair = (core_half(left, index), right) if dim == 0 else (left, core_half(right, index))
            return dot(*pair, ((0,), (0,)))

        came = swap(term(1 - core).astype(BF16), "core", 2, 1)
        return (term(core) + came.astype(F32)).astype(BF16)

    def settle(held, dim):
        return lax.psum_scatter(held, "ctx", scatter_dimension=dim, tiled=True)

    def own_rows(summed, dim):
        return over_y(lambda index: lax.dynamic_slice_in_dim(summed, index * rows, rows, axis=dim))

    def gain_settle(grads):
        def add(values, axis, size):
            step = 1
            while step < size:
                values = values + swap(values, axis, size, step)
                step *= 2
            return values

        grads = add(add(add(grads, group, nq), "core", 2), "ctx", nc)
        return pick(grads.reshape(2, 2 * nc * ny, rows), (core * nc + ctx) * ny + yi, 1)

    head_cols = w_query.shape[1] // ny
    hidden_cols = w_gate.shape[1] // ny
    part_cols = hidden_cols // MLP_CHUNKS
    out_turned, down_turned = w_out.T, w_down.T
    wanted = [[(w, 0, head_cols) for w in (w_query, w_key, w_value, out_turned)]]
    tile = min(TILE, part_cols)
    tiles = part_cols // tile
    for part in range(MLP_CHUNKS):
        start = part * part_cols
        wanted.append(
            [(w, start + i * tile, tile) for i in range(tiles) for w in (w_gate, w_up)]
            + [(down_turned, start, part_cols)]
        )

    def prepare(sources, *before):
        def block(index):
            return after(jnp.concatenate([columns(w, index, *p) for w, *p in sources], axis=1), *before)

        return jnp.concatenate(over_y(block), axis=0)

    held = prepare(wanted[0])
    x_rows = rows_for(after(tokens, held))
    weights = [fetch(held)]
    x_low = turn(x_rows)
    for sources in wanted[1:]:
        held = prepare(sources, held, x_rows)
        weights.append(fetch(held))
    qkv_weight, out_weight = weights[0][:, : 3 * head_cols], weights[0][:, 3 * head_cols :]

    gains = jnp.concatenate([attn_gain, mlp_gain])[None]
    for axis, size, index in (("y", ny, yi), ("ctx", nc, ctx), ("core", 2, core)):
        step = 1
        while step < size:
            other = swap(gains, axis, size, step)
            odd = (index & step) != 0
            gains = jnp.concatenate([jnp.where(odd, other, gains), jnp.where(odd, gains, other)])
            step *= 2
    gain_one = gains[:, :rows].reshape(width).astype(F32)
    gain_two = gains[:, rows:].reshape(width).astype(F32)

    seg_parts = [segments] + [swap(segments, "y", ny, step) for step in range(1, ny)]
    all_segments = jnp.concatenate(by_index(seg_parts, yi), axis=0)
    starts = doc_starts(pick(all_segments, ctx, 0))
    cosine, sine = rope_tables(starts)
    starts = jnp.broadcast_to(starts[:, None], (length, PAIR))

    x_low, normed_piece = run_norm_forward([x_low], gain_one, BF16, inward)
    normed = gather_rows(normed_piece)
    up_piece = run_add_rows([turn(rows_for(after(cotangent, x_low)))], inward)
    upstream = gather_rows(after(up_piece, normed))

    qkv = dot(normed, qkv_weight, ((1,), (0,)))
    attended, logs = run_attention_forward(qkv, cosine, sine, starts)
    attn_terms = row_terms(dot(attended, out_weight, ((1,), (1,))).astype(BF16))
    residual, normed_two = run_norm_forward([x_low] + attn_terms, gain_two, F32)
    normed_two = gather_rows(normed_two)

    mlp_out = None
    back_two = None
    mlp_sums = []
    wait_for = []
    now_two = normed_two
    for part in range(MLP_CHUNKS):
        weight = weights[1 + part]
        gate_up, down = weight[:, : 2 * part_cols], weight[:, 2 * part_cols :]
        hidden, both_grad = run_feed_forward(now_two, upstream, weight, part_cols)
        term = dot(both_grad, gate_up, ((1,), (1,)))
        back_two = term if back_two is None else back_two + term
        if part + 1 == MLP_CHUNKS:
            back_two = back_two.astype(BF16)
            hidden, both_grad = after(hidden, back_two), after(both_grad, back_two)
        held_both, held_down = partials(normed_two, both_grad, 0), partials(hidden, upstream, 1)
        sums = [(settle(held_down, 1), 1), (settle(held_both, 0), 0)]
        if part + 1 < MLP_CHUNKS:
            now_two = after(now_two, held_both, held_down)
            wait_for += [summed for summed, _ in sums]
        mlp_sums.append(sums)
        term = dot(hidden, down, ((1,), (1,)))
        mlp_out = term if mlp_out is None else mlp_out + term

    mlp_out = mlp_out.astype(BF16)
    back_terms = row_terms(back_two, held_both, held_down, mlp_out)
    back_terms[0] = after(back_terms[0], *wait_for)
    gain_two_grad, (residual_grad, residual_low) = run_norm_backward(
        back_terms, residual, gain_two, up_piece, [F32, BF16], COST
    )
    residual_low = gather_rows(residual_low)
    attended_grad = dot(residual_low, out_weight, ((1,), (0,))).astype(BF16)
    qkv_grad = run_attention_backward(qkv, attended_grad, logs, cosine, sine, starts)
    attn_held = jnp.concatenate(
        [partials(normed, qkv_grad, 0), partials(residual_low, after(attended, attended_grad), 0)], axis=1
    )
    attn_summed = settle(attn_held, 0)
    back_one = run_turned_product(after(qkv_grad, attn_held, *[t for t, _ in mlp_sums[-1]]), weights[0])
    one_terms = row_terms(back_one)
    mlp_terms = row_terms(after(mlp_out, residual_low), attn_held)
    block_out = turn(run_add_rows([after(residual, back_one)] + mlp_terms, outward))
    received = jax.tree.leaves(one_terms)
    one_terms[0] = after(one_terms[0], attn_summed)
    gain_one_grad, (inputs_grad,) = run_norm_backward(
        one_terms, x_low, gain_one, residual_grad, [BF16], SHORT, outward
    )
    turned = turn(inputs_grad)
    block_out = pieces_out(after(block_out, inputs_grad))
    gain_grads = gain_settle(
        after(jnp.concatenate([gain_one_grad, gain_two_grad]), turned)
    )
    mlp_grads = []
    for part, pair in enumerate(mlp_sums):
        ready = [back_one] if part + 1 < MLP_CHUNKS else received
        mlp_grads.append([own_rows(after(summed, *ready), dim) for summed, dim in pair])
    grad_tokens = pieces_out(turned)
    attn_grads = own_rows(attn_summed, 0)
    grad_tokens = after(grad_tokens, *attn_grads).astype(F32)

    grad_query, grad_key, grad_value = (
        jnp.concatenate(
            [p[:, i * head_cols : (i + 1) * head_cols] for p in attn_grads], axis=1
        ).astype(F32)
        for i in range(3)
    )
    grad_out = jnp.concatenate([p[:, 3 * head_cols :] for p in attn_grads], axis=1).T.astype(F32)
    grad_gate, grad_up = (
        jnp.concatenate(
            [
                pair[-1][y][:, (2 * j + i) * tile : (2 * j + i + 1) * tile]
                for y in range(ny)
                for pair in mlp_grads
                for j in range(tiles)
            ],
            axis=1,
        ).astype(F32)
        for i in range(2)
    )
    grad_down = jnp.concatenate(
        [pair[0][y] for y in range(ny) for pair in mlp_grads], axis=0
    ).astype(F32)
    return (
        block_out,
        grad_tokens,
        gain_grads[0],
        grad_query,
        grad_key,
        grad_value,
        grad_out,
        gain_grads[1],
        grad_gate,
        grad_up,
        grad_down,
    )


def solution(mesh):
    ny, nc, nx = mesh.shape["fsdp"] // 2, mesh.shape["ctx"], mesh.shape["tensor"]
    fine = Mesh(mesh.devices.reshape(ny, 2, nc, nx), ("y", "core", "ctx", "tensor"))
    fsdp = ("y", "core")
    owner = ("y", "core", "ctx")
    token_spec = P(fsdp, "ctx", None)
    weight_specs = (
        P(owner),
        P(owner, "tensor"),
        P(owner, "tensor"),
        P(owner, "tensor"),
        P("tensor", owner),
        P(owner),
        P(owner, "tensor"),
        P(owner, "tensor"),
        P("tensor", owner),
    )
    return jax.shard_map(
        functools.partial(per_device, (ny, nc, nx)),
        mesh=fine,
        in_specs=(token_spec, P(fsdp, None), token_spec) + weight_specs,
        out_specs=(token_spec, token_spec) + weight_specs,
        check_vma=False,
    )
```
